32 devices in a mesh: rad: 4 (over y, core), ax: 8 (over z, x).
Axes of the slice: x: 2, y: 2, z: 4, core: 2. Of those that a mesh axis runs over, the one named last changes fastest.
Arguments:
- charge: float32 [64, 128, 128], P('rad', 'ax'), may hold values from -6 to 6
- density: float32 [64, 128, 128], P('rad', 'ax'), may hold values from 0.1 to 20
- previous: float32 [64, 128, 128], P('rad', 'ax'), may hold values from -4 to 4
- levels: int32 [4, 8, 8], P('rad', 'ax'), may hold values from 0 to 2
Outputs:
- potential: float32 [64, 128, 128], P('rad', 'ax')
The draws below stay inside these ranges and needn't reach their ends.
All inputs are finite; a program needn't handle non-finite values.
Results may differ from the reference program's by a relative error of at most 0.0003.
Values sent between devices are 32-bit elements; how exact they have to be, the bound alone decides.
A program may use at most 64 MiB of HBM per device.

```python
import math
import jax
import jax.numpy as jnp
from jax import lax

W = 128
PATCH = 16
NU = 2
EXTRA = 2
CS = 8
NR = 64
NA = 128


two_pi = 2.0 * math.pi


def wave_sum(key, count, lowest, highest):
    radial_pos = (jnp.arange(NR, dtype=jnp.float32) / NR)[:, None, None]
    axial_pos = (jnp.arange(NA, dtype=jnp.float32) / NA)[None, :, None]
    depth_pos = (jnp.arange(W, dtype=jnp.float32) / W)[None, None, :]
    total = jnp.zeros((NR, NA, W), jnp.float32)
    for number in range(count):
        subkeys = jax.random.split(jax.random.fold_in(key, number), 6)
        radial_wave = jax.random.randint(subkeys[0], (), 1, 3).astype(jnp.float32)
        axial_wave = jax.random.randint(subkeys[1], (), 1, 5).astype(jnp.float32)
        depth_wave = jax.random.randint(subkeys[2], (), 0, 3).astype(jnp.float32)
        phases = jax.random.uniform(subkeys[3], (3,), jnp.float32, 0.0, two_pi)
        height = jax.random.uniform(subkeys[4], (), jnp.float32, lowest, highest)
        flip = (2 * jax.random.randint(subkeys[5], (), 0, 2) - 1).astype(jnp.float32)
        radial_part = jnp.sin(two_pi * radial_wave * radial_pos + phases[0])
        axial_part = jnp.sin(two_pi * axial_wave * axial_pos + phases[1])
        depth_part = jnp.cos(two_pi * depth_wave * depth_pos + phases[2])
        total = total + flip * height * radial_part * axial_part * depth_part
    return total


def draw_charge(key, part):
    base_key = jax.random.fold_in(key, 11)
    noise_key, wave_key = jax.random.split(base_key)
    rough = jnp.clip(jax.random.normal(noise_key, (NR, NA, W), jnp.float32), -4.0, 4.0)
    smooth = wave_sum(wave_key, 4, 0.15, 0.3)
    return rough + smooth


def draw_previous(key, part):
    base_key = jax.random.fold_in(key, 23)
    noise_key, wave_key = jax.random.split(base_key)
    rough = 0.3 * jnp.clip(jax.random.normal(noise_key, (NR, NA, W), jnp.float32), -4.0, 4.0)
    return rough + wave_sum(wave_key, 3, 0.4, 0.9)


def plant(array, stream_key, least, largest):
    longest = array.shape.index(max(array.shape))
    spots = []
    for shift in (0, 1):
        where = [jax.random.randint(jax.random.fold_in(stream_key, axis), (), 0, length) for axis, length in enumerate(array.shape)]
        where[longest] = (where[longest] + shift) % array.shape[longest]
        spots.append(tuple(where))
    return array.at[spots[0]].set(least).at[spots[1]].set(largest)


def block_scale(own_key, dims, shards, least, largest):
    loudness = 1.0
    for dim, blocks in shards:
        draws = jax.random.uniform(jax.random.fold_in(jax.random.fold_in(own_key, 6), dim), (blocks,), jnp.float32, least / len(shards), largest / len(shards))
        loudness = loudness * jnp.repeat(jnp.exp(draws), dims[dim] // blocks).reshape((-1,) + (1,) * (len(dims) - 1 - dim))
    return loudness


def setup_inputs(seed: int = 0) -> dict:
    streams_of = jax.random.split(jax.random.key(seed), 5)
    return {
        "charge": draw_charge(jax.random.fold_in(streams_of[4], 71), 0),
        "density": jnp.clip(jnp.exp(math.log(20.0) - 5.2983174 * jax.random.uniform(streams_of[1], (NR, NA, W), jnp.float32) ** block_scale(streams_of[1], (NR, NA, W), ((0, 4), (1, 8)), -0.2, 0.2)), 0.1, 20.0),
        "previous": draw_previous(jax.random.fold_in(streams_of[4], 71), 0),
        "levels": plant(jax.random.randint(streams_of[3], (NR // PATCH, NA // PATCH, W // PATCH), 0, 3), jax.random.fold_in(streams_of[3], 1), 0, 2).astype(jnp.int32),
    }


drift_factor = 0.5


def coefficients(padded, scale):
    centre = padded[1:-1, 1:-1, 1:-1]
    faces = (
        0.5 * (centre + padded[:-2, 1:-1, 1:-1]) * scale,
        0.5 * (centre + padded[2:, 1:-1, 1:-1]) * scale,
        0.5 * (centre + padded[1:-1, :-2, 1:-1]) * scale,
        0.5 * (centre + padded[1:-1, 2:, 1:-1]) * scale,
        0.5 * (centre + padded[1:-1, 1:-1, :-2]) * scale,
        0.5 * (centre + padded[1:-1, 1:-1, 2:]) * scale,
    )
    return faces, faces[0] + faces[1] + faces[2] + faces[3] + faces[4] + faces[5]


def neighbour_sum(padded, faces):
    total = faces[0] * padded[:-2, 1:-1, 1:-1] + faces[1] * padded[2:, 1:-1, 1:-1]
    total = total + faces[2] * padded[1:-1, :-2, 1:-1] + faces[3] * padded[1:-1, 2:, 1:-1]
    return total + faces[4] * padded[1:-1, 1:-1, :-2] + faces[5] * padded[1:-1, 1:-1, 2:]


def parity(shape):
    total = lax.broadcasted_iota(jnp.int32, shape, 0) + lax.broadcasted_iota(jnp.int32, shape, 1)
    total = total + lax.broadcasted_iota(jnp.int32, shape, 2)
    return total % 2 == 0


def pad_whole(values):
    return jnp.pad(values, 1)


def relax(field, source, operator, red, mask, padder):
    faces, diagonal = operator
    for colour in (red, jnp.logical_not(red)):
        update = (source + neighbour_sum(padder(field), faces)) / diagonal
        field = jnp.where(jnp.logical_and(colour, mask), update, field)
    return field


def residual_of(field, source, operator, padder):
    faces, diagonal = operator
    return source - (diagonal * field - neighbour_sum(padder(field), faces))


def restrict(values):
    rows, cols, depth = values.shape
    return values.reshape(rows // 2, 2, cols // 2, 2, depth // 2, 2).mean(axis=(1, 3, 5))


def prolong(values):
    return jnp.repeat(jnp.repeat(jnp.repeat(values, 2, axis=0), 2, axis=1), 2, axis=2)


def reference(charge, density, previous, levels):
    eps0 = 1.0 + drift_factor * density
    operator0 = coefficients(pad_whole(eps0), 1.0)
    red0 = parity(charge.shape)
    field = previous
    for sweep in range(NU):
        field = relax(field, charge, operator0, red0, True, pad_whole)
    refined = jnp.repeat(jnp.repeat(jnp.repeat(levels, PATCH, axis=0), PATCH, axis=1), PATCH, axis=2)
    for sweep in range(EXTRA):
        field = relax(field, charge, operator0, red0, refined > sweep, pad_whole)
    source1 = restrict(residual_of(field, charge, operator0, pad_whole))
    eps1 = restrict(eps0)
    operator1 = coefficients(pad_whole(eps1), 0.25)
    red1 = parity(source1.shape)
    middle = jnp.zeros_like(source1)
    for sweep in range(NU):
        middle = relax(middle, source1, operator1, red1, True, pad_whole)
    source2 = restrict(residual_of(middle, source1, operator1, pad_whole))
    eps2 = restrict(eps1)
    operator2 = coefficients(pad_whole(eps2), 0.0625)
    red2 = parity(source2.shape)
    coarse = jnp.zeros_like(source2)
    for sweep in range(CS):
        coarse = relax(coarse, source2, operator2, red2, True, pad_whole)
    middle = middle + prolong(coarse)
    for sweep in range(NU):
        middle = relax(middle, source1, operator1, red1, True, pad_whole)
    field = field + prolong(middle)
    for sweep in range(NU):
        field = relax(field, charge, operator0, red0, True, pad_whole)
    return field
```

```python
import jax
import jax.numpy as jnp
from jax import lax
from jax.experimental import pallas as pl
from jax.experimental.pallas import tpu as pltpu
from jax.sharding import PartitionSpec as P

NU = 2
EXTRA = 2
CS = 8
PATCH = 16
MESH = pl.DeviceIdType.MESH
NX = 24


def make_kernel(nrad, nax):
    nd = nrad * nax

    def kernel(charge, density, previous, levels, out, v, e, co, g0, d0, tmp, src1, m, e1, co1, g1, d1,
               st, hal, gat, eg, cg, sg, f2, send_sem, recv_sem, gsend, grecv):
        R, A, W = 16, 16, 128
        ri, ai = lax.axis_index("rad"), lax.axis_index("ax")
        me = ri * nax + ai
        has = (ri > 0, ri < nrad - 1, ai > 0, ai < nax - 1)
        nbr = ((ri - 1, ai), (ri + 1, ai), (ri, ai - 1), (ri, ai + 1))
        opp = (1, 0, 3, 2)

        barrier = pltpu.get_barrier_semaphore()

        def greet(i, c):
            @pl.when(i != me)
            def _():
                pl.semaphore_signal(barrier, inc=1, device_id=(i // nax, i % nax), device_id_type=MESH)
            return c

        lax.fori_loop(0, nd, greet, 0)
        zero = jnp.zeros((16, 128), jnp.float32)
        for d in range(4):
            @pl.when(jnp.logical_not(has[d]))
            def _(d=d):
                for x in range(NX):
                    hal[x, d] = zero

        def copy(x, d, n, to_slot):
            return pltpu.make_async_remote_copy(
                src_ref=st.at[x, d, pl.ds(0, n)], dst_ref=hal.at[x, to_slot, pl.ds(0, n)],
                send_sem=send_sem.at[x, d], recv_sem=recv_sem.at[x, to_slot],
                device_id=nbr[d], device_id_type=MESH)

        used = {}

        def send(x, ref, n):
            used[x] = n
            st[x, 0, 0:n] = ref[1]
            st[x, 1, 0:n] = ref[n]
            st[x, 2, 0:n] = ref[1:n + 1, 0, :]
            st[x, 3, 0:n] = ref[1:n + 1, n - 1, :]
            for d in range(4):
                @pl.when(has[d])
                def _(d=d):
                    copy(x, d, n, opp[d]).start()

        def recv(x, ref, n):
            for d in range(4):
                @pl.when(has[d])
                def _(d=d):
                    copy(x, d, n, d).wait_recv()
            ref[0] = hal[x, 0, 0:n]
            ref[n + 1] = hal[x, 1, 0:n]

        def shifts(ref, x, r, n, step):
            c = ref[r + 1]
            sub = lax.broadcasted_iota(jnp.int32, (n, 128), 0)
            left = pltpu.roll(c, 1, 0)
            right = pltpu.roll(c, n - 1, 0)
            hl = 0.0 if x is None else hal[x, 2, r:r + 1]
            hr = 0.0 if x is None else hal[x, 3, r:r + 1]
            left = jnp.where(sub == 0, hl, left)
            right = jnp.where(sub == n - 1, hr, right)
            return c, (ref[r], ref[r + 2], left, right, pltpu.roll(c, step, 1), pltpu.roll(c, 128 - step, 1))

        def coefs(ref, x, n, step, scale, cref, gref, dref, source):
            lane = lax.broadcasted_iota(jnp.int32, (n, 128), 1)
            for r in range(n):
                c, (u, dn, l, rt, wl, wr) = shifts(ref, x, r, n, step)
                wl = jnp.where(lane < step, 0.0, wl)
                wr = jnp.where(lane >= 128 - step, 0.0, wr)
                diag = (6.0 * c + u + dn + l + rt + wl + wr) * (0.5 * scale)
                inv = 1.0 / diag
                h = inv * (0.5 * scale)
                cref[0, r] = (c + u) * h
                cref[1, r] = (c + dn) * h
                cref[2, r] = (c + l) * h
                cref[3, r] = (c + rt) * h
                cref[4, r] = jnp.where(lane < step, 0.0, (c + wl) * h)
                cref[5, r] = jnp.where(lane >= 128 - step, 0.0, (c + wr) * h)
                dref[r] = diag
                if source is not None:
                    gref[r] = source[r] * inv

        def update(ref, x, r, n, step, cref, gref):
            c, nb = shifts(ref, x, r, n, step)
            t = (gref[r] + cref[0, r] * nb[0]) + cref[1, r] * nb[1]
            s = cref[2, r] * nb[2] + cref[3, r] * nb[3]
            q = cref[4, r] * nb[4] + cref[5, r] * nb[5]
            return c, t + (s + q)

        def parity_of(n, step):
            return (lax.broadcasted_iota(jnp.int32, (n, 128), 0)
                    + lax.broadcasted_iota(jnp.int32, (n, 128), 1) // step) % 2

        def half(ref, x, n, step, cref, gref, colour, mask=None):
            par = parity_of(n, step)
            ms = [par == colour, par == 1 - colour]
            if mask is not None:
                ms = [jnp.logical_and(k, mask) for k in ms]
            for r in range(n):
                c, new = update(ref, x, r, n, step, cref, gref)
                ref[r + 1] = jnp.where(ms[r % 2], new, c)

        for r in range(R):
            e[r + 1] = 1.0 + 0.5 * density[r]
            v[r + 1] = previous[r]
        pl.semaphore_wait(barrier, nd - 1)
        send(0, e, R)
        send(1, v, R)
        lane16 = lax.broadcasted_iota(jnp.int32, (16, 128), 1)
        lev = jnp.zeros((16, 128), jnp.int32)
        for p in range(8):
            lev = jnp.where(lane16 // PATCH == p, levels[0, 0, p], lev)

        lane8 = lax.broadcasted_iota(jnp.int32, (8, 128), 1)
        sub8 = lax.broadcasted_iota(jnp.int32, (8, 128), 0)

        def pairs(x, lane, w):
            n = x.shape[0]
            return x + jnp.where(lane % (2 * w) < w, pltpu.roll(x, 128 - w, 1), pltpu.roll(x, w, 1))

        for q in range(8):
            tmp[q] = e[2 * q + 1] + e[2 * q + 2]
        for q in range(8):
            s = tmp[q, pl.ds(0, 8, stride=2), :] + tmp[q, pl.ds(1, 8, stride=2), :]
            e1[q + 1] = pairs(s, lane8, 1) * 0.125
        send(2, e1, 8)

        recv(0, e, R)
        coefs(e, 0, R, 1, 1.0, co, g0, d0, charge)
        recv(1, v, R)
        x = 1
        nxt = 3
        for sweep in range(NU + EXTRA):
            mask = None if sweep < NU else lev > (sweep - NU)
            for colour in range(2):
                half(v, x, R, 1, co, g0, colour, mask)
                x = nxt
                nxt += 1
                send(x, v, R)
                if sweep == 0 and colour == 0:
                    recv(2, e1, 8)
                    coefs(e1, 2, 8, 2, 0.25, co1, None, d1, None)
                recv(x, v, R)
        for q in range(8):
            rs = []
            for r in (2 * q, 2 * q + 1):
                c, new = update(v, x, r, R, 1, co, g0)
                rs.append(d0[r] * (new - c))
            tmp[q] = rs[0] + rs[1]
        for q in range(8):
            s = tmp[q, pl.ds(0, 8, stride=2), :] + tmp[q, pl.ds(1, 8, stride=2), :]
            g1[q] = pairs(s, lane8, 1) * 0.125 / d1[q]
        par = parity_of(8, 2)
        m[0] = zero[:8]
        m[9] = zero[:8]
        for r in range(8):
            m[r + 1] = jnp.where(par == r % 2, g1[r], 0.0)
        for i in range(1, 2 * NU + 1):
            x = nxt
            nxt += 1
            send(x, m, 8)
            recv(x, m, 8)
            if i < 2 * NU:
                half(m, x, 8, 2, co1, g1, i % 2)
        for q in range(4):
            rs = []
            for r in (2 * q, 2 * q + 1):
                c, new = update(m, x, r, 8, 2, co1, g1)
                rs.append(d1[r] * (new - c))
            tmp[q, 0:8] = rs[0] + rs[1]
            tmp[q, 8:16] = e1[2 * q + 1] + e1[2 * q + 2]
        lane1 = lax.broadcasted_iota(jnp.int32, (1, 128), 1)
        for k in range(2):
            for q in range(4):
                y = tmp[q, 8 * k:8 * k + 8]
                y = pairs(y, lane8, 2)
                tmp[q, 8 * k:8 * k + 8] = y
        for k in range(2):
            for q in range(4):
                p = jnp.zeros((1, 128), jnp.float32)
                for j in range(4):
                    a = 8 * k + 2 * j
                    p = jnp.where(lane1 % 4 == j, tmp[q, a:a + 1] + tmp[q, a + 1:a + 2], p)
                gat[me, pl.ds(4 * k + q, 1)] = p * 0.125

        def gcopy(i):
            return pltpu.make_async_remote_copy(
                src_ref=gat.at[me], dst_ref=gat.at[me], send_sem=gsend, recv_sem=grecv,
                device_id=(i // nax, i % nax), device_id_type=MESH)

        def scatter(i, c):
            @pl.when(i != me)
            def _():
                gcopy(i).start()
            return c

        lax.fori_loop(0, nd, scatter, 0)
        pltpu.make_async_remote_copy(
            src_ref=gat.at[pl.ds(0, nd - 1)], dst_ref=gat.at[pl.ds(0, nd - 1)], send_sem=gsend, recv_sem=grecv,
            device_id=nbr[0], device_id_type=MESH).wait_recv()

        n2 = nrad * 4
        zc = jnp.zeros((nax, 128), jnp.float32)
        sub = lax.broadcasted_iota(jnp.int32, (nax, 128), 0)
        lane = lax.broadcasted_iota(jnp.int32, (nax, 128), 1)
        j4 = lane % 4

        def around(c):
            lf = jnp.where(j4 == 0, pltpu.roll(pltpu.roll(c, 125, 1), 1, 0), pltpu.roll(c, 1, 1))
            rt = jnp.where(j4 == 3, pltpu.roll(pltpu.roll(c, 3, 1), nax - 1, 0), pltpu.roll(c, 127, 1))
            return lf, rt, pltpu.roll(c, 4, 1), pltpu.roll(c, 124, 1)

        first = jnp.logical_and(sub == 0, j4 == 0)
        last = jnp.logical_and(sub == nax - 1, j4 == 3)
        low = lane < 4
        high = lane >= 124
        eg[0] = zc
        eg[n2 + 1] = zc
        f2[0] = zc
        f2[n2 + 1] = zc
        for r in range(n2):
            eg[r + 1] = gat[(r // 4) * nax:(r // 4 + 1) * nax, 4 + r % 4, :]
            f2[r + 1] = zc

        def coarse_coefs(r, _):
            c = eg[r + 1]
            lf, rt, wl, wr = around(c)
            lf = jnp.where(first, 0.0, lf)
            rt = jnp.where(last, 0.0, rt)
            wl = jnp.where(low, 0.0, wl)
            wr = jnp.where(high, 0.0, wr)
            u, dn = eg[r], eg[r + 2]
            t = 6.0 * c + u + dn + lf + rt + wl + wr
            h = 1.0 / t
            cg[0, r] = (c + u) * h
            cg[1, r] = (c + dn) * h
            cg[2, r] = jnp.where(first, 0.0, (c + lf) * h)
            cg[3, r] = jnp.where(last, 0.0, (c + rt) * h)
            cg[4, r] = jnp.where(low, 0.0, (c + wl) * h)
            cg[5, r] = jnp.where(high, 0.0, (c + wr) * h)
            sg[r] = h * 32.0
            return 0

        for r in range(n2):
            coarse_coefs(r, 0)
            sg[r] = sg[r] * gat[(r // 4) * nax:(r // 4 + 1) * nax, r % 4, :]
        par2 = (j4 + lane // 4) % 2

        def coarse_sweep(k, _):
            for colour in range(2):
                for r in range(n2):
                    c = f2[r + 1]
                    lf, rt, wl, wr = around(c)
                    t = sg[r] + cg[0, r] * f2[r] + cg[1, r] * f2[r + 2]
                    t = t + (cg[2, r] * lf + cg[3, r] * rt) + (cg[4, r] * wl + cg[5, r] * wr)
                    f2[r + 1] = jnp.where(par2 == (colour + r) % 2, t, c)
            return 0

        lax.fori_loop(0, CS, coarse_sweep, 0)

        m4 = lane8 % 4
        for q in range(4):
            own = jnp.broadcast_to(f2[4 * ri + q + 1, pl.ds(ai, 1), :], (8, 128))
            t = jnp.zeros((8, 128), jnp.float32)
            want = sub8 // 2 - m4
            for s in range(-3, 4):
                t = jnp.where(want == s, own if s == 0 else pltpu.roll(own, (-s) % 128, 1), t)
            m[2 * q + 1] = m[2 * q + 1] + t
            m[2 * q + 2] = m[2 * q + 2] + t
        for i in range(2 * NU):
            x = nxt
            nxt += 1
            send(x, m, 8)
            recv(x, m, 8)
            half(m, x, 8, 2, co1, g1, i % 2)
        for q in range(8):
            y = m[q + 1]
            tmp[q, pl.ds(0, 8, stride=2), :] = y
            tmp[q, pl.ds(1, 8, stride=2), :] = y
        for r in range(R):
            v[r + 1] = v[r + 1] + tmp[r // 2]
        for i in range(2 * NU):
            x = nxt
            nxt += 1
            send(x, v, R)
            recv(x, v, R)
            half(v, x, R, 1, co, g0, i % 2)
        out[...] = v[1:R + 1]
        assert nxt <= NX
        for d in range(4):
            @pl.when(has[d])
            def _(d=d):
                for x, n in used.items():
                    copy(x, d, n, opp[d]).wait_send()
        pltpu.make_async_remote_copy(
            src_ref=gat.at[pl.ds(0, nd - 1)], dst_ref=gat.at[pl.ds(0, nd - 1)], send_sem=gsend, recv_sem=grecv,
            device_id=nbr[0], device_id_type=MESH).wait_send()

    return kernel


def solution(mesh):
    nrad, nax = mesh.shape["rad"], mesh.shape["ax"]
    nd = nrad * nax
    n2 = nrad * 4
    f32 = jnp.float32

    def on_device(charge, density, previous, levels):
        vm = pl.BlockSpec(memory_space=pltpu.VMEM)
        return pl.pallas_call(
            make_kernel(nrad, nax),
            out_shape=jax.ShapeDtypeStruct(charge.shape, f32),
            in_specs=[vm, vm, vm, pl.BlockSpec(memory_space=pltpu.SMEM)],
            out_specs=vm,
            scratch_shapes=[
                pltpu.VMEM((18, 16, 128), f32),
                pltpu.VMEM((18, 16, 128), f32),
                pltpu.VMEM((6, 16, 16, 128), f32),
                pltpu.VMEM((16, 16, 128), f32),
                pltpu.VMEM((16, 16, 128), f32),
                pltpu.VMEM((8, 16, 128), f32),
                pltpu.VMEM((8, 8, 128), f32),
                pltpu.VMEM((10, 8, 128), f32),
                pltpu.VMEM((10, 8, 128), f32),
                pltpu.VMEM((6, 8, 8, 128), f32),
                pltpu.VMEM((8, 8, 128), f32),
                pltpu.VMEM((8, 8, 128), f32),
                pltpu.VMEM((NX, 4, 16, 128), f32),
                pltpu.VMEM((NX, 4, 16, 128), f32),
                pltpu.VMEM((nd, 8, 128), f32),
                pltpu.VMEM((n2 + 2, nax, 128), f32),
                pltpu.VMEM((6, n2, nax, 128), f32),
                pltpu.VMEM((n2, nax, 128), f32),
                pltpu.VMEM((n2 + 2, nax, 128), f32),
                pltpu.SemaphoreType.DMA((NX, 4)),
                pltpu.SemaphoreType.DMA((NX, 4)),
                pltpu.SemaphoreType.DMA,
                pltpu.SemaphoreType.DMA,
            ],
            compiler_params=pltpu.CompilerParams(
                collective_id=0, has_side_effects=True, vmem_limit_bytes=40 * 2**20),
        )(charge, density, previous, levels)

    return jax.shard_map(
        on_device, mesh=mesh,
        in_specs=(P("rad", "ax", None),) * 4,
        out_specs=P("rad", "ax", None), check_vma=False)
```

```python
import jax
import jax.numpy as jnp
from jax import lax
from jax.experimental import pallas as pl
from jax.experimental.pallas import tpu as pltpu
from jax.sharding import PartitionSpec as P

NU = 2
EXTRA = 2
CS = 8
PATCH = 16
MESH = pl.DeviceIdType.MESH
NX = 9
DIRS = ((-1, 0), (1, 0), (0, -1), (0, 1), (-1, -1), (1, 1), (-1, 1), (1, -1))
OPP = (1, 0, 3, 2, 5, 4, 7, 6)
H0 = 5
H1 = 6
PAD = 4


def make_kernel(nrad, nax):
    nd = nrad * nax

    def kernel(charge, density, previous, levels, out,
               de, e, ch, va, vb, vc, co, g0, d0, tmp, lv, e1, s1, m, m2, co1, h1, d1,
               gat, eg, cg, sg, f2, send_sem, recv_sem, gsend, grecv):
        ri, ai = lax.axis_index("rad"), lax.axis_index("ax")
        me = ri * nax + ai
        lo_r, hi_r, lo_a, hi_a = ri > 0, ri < nrad - 1, ai > 0, ai < nax - 1
        okr = {-1: lo_r, 1: hi_r, 0: None}
        oka = {-1: lo_a, 1: hi_a, 0: None}
        has = []
        for dr, da in DIRS:
            x, y = okr[dr], oka[da]
            has.append(y if x is None else x if y is None else jnp.logical_and(x, y))

        barrier = pltpu.get_barrier_semaphore()

        def greet(i, c):
            @pl.when(i != me)
            def _():
                pl.semaphore_signal(barrier, inc=1, device_id=(i // nax, i % nax), device_id_type=MESH)
            return c

        lax.fori_loop(0, nd, greet, 0)

        def region(dst, h, n, k, d):
            dr, da = DIRS[d]
            rows = {-1: (h - k, k), 0: (h, n), 1: (h + n, k)}[dr]
            cols = {-1: (0, 8), 0: (8, n), 1: (8 + n, 8)}[da]
            return dst.at[pl.ds(*rows), pl.ds(*cols)]

        def face(src, off, n, k, d):
            dr, da = DIRS[d]
            rows = {-1: (off[0], k), 0: (off[0], n), 1: (off[0] + n - k, k)}[dr]
            cols = {-1: (off[1], 8), 0: (off[1], n), 1: (off[1] + n - 8, 8)}[da]
            return src.at[pl.ds(*rows), pl.ds(*cols)]

        OWN0, OWN1 = (H0, 8), (H1, 8)
        plan = {
            0: (density, (0, 0), de, H0, 16, 5),
            1: (previous, (0, 0), va, H0, 16, 4),
            2: (charge, (0, 0), ch, H0, 16, 4),
            4: (e1, OWN1, e1, H1, 8, 6),
            5: (va, OWN0, vb, H0, 16, 5),
            6: (s1, OWN1, s1, H1, 8, 5),
            7: (vb, OWN0, vc, H0, 16, 4),
            8: (m, OWN1, m2, H1, 8, 6),
        }

        def copy(x, d, slot):
            dr, da = DIRS[d]
            if x == 3:
                src, dst = lv.at[8], lv.at[slot]
            else:
                source, off, dest, h, n, k = plan[x]
                src, dst = face(source, off, n, k, d), region(dest, h, n, k, slot)
            return pltpu.make_async_remote_copy(
                src_ref=src, dst_ref=dst, send_sem=send_sem.at[x, d], recv_sem=recv_sem.at[x, slot],
                device_id=(ri + dr, ai + da), device_id_type=MESH)

        def send(x):
            for d in range(8):
                @pl.when(has[d])
                def _(d=d):
                    copy(x, d, OPP[d]).start()

        def recv(x):
            for d in range(8):
                @pl.when(has[d])
                def _(d=d):
                    if x == 3:
                        copy(x, d, d).wait_recv()
                    else:
                        dest, h, n, k = plan[x][2:]
                        dst = region(dest, h, n, k, d)
                        pltpu.make_async_remote_copy(
                            src_ref=dst, dst_ref=dst, send_sem=send_sem.at[x, d], recv_sem=recv_sem.at[x, d],
                            device_id=(ri + DIRS[d][0], ai + DIRS[d][1]), device_id_type=MESH).wait_recv()

        for d in range(8):
            @pl.when(jnp.logical_not(has[d]))
            def _(d=d):
                for x, (_s, _o, dest, h, n, k) in plan.items():
                    ref = region(dest, h, n, k, d)
                    ref[...] = jnp.zeros(ref.shape, jnp.float32)
                lv[d] = jnp.zeros((8, 128), jnp.int32)

        lane8 = lax.broadcasted_iota(jnp.int32, (8, 128), 1)
        sub8 = lax.broadcasted_iota(jnp.int32, (8, 128), 0)
        lev = jnp.zeros((8, 128), jnp.int32)
        for p in range(8):
            lev = jnp.where(lane8 // PATCH == p, levels[0, 0, p], lev)
        lv[8] = lev
        pl.semaphore_wait(barrier, nd - 1)
        send(0)
        send(2)
        send(1)
        send(3)

        def inside(n):
            sub = lax.broadcasted_iota(jnp.int32, (n + 16, 128), 0)
            left, right = lo_a.astype(jnp.float32), hi_a.astype(jnp.float32)
            row = jnp.where(sub < 8, left, jnp.where(sub >= n + 8, right, 1.0))
            return [row * lo_r.astype(jnp.float32), row, row * hi_r.astype(jnp.float32)]

        def zone(r, n):
            return 0 if r < 0 else 2 if r >= n else 1

        def shifts(ref, h, r, n, step):
            c = ref[r + h]
            return c, (ref[r + h - 1], ref[r + h + 1], pltpu.roll(c, 1, 0), pltpu.roll(c, n + 15, 0),
                       pltpu.roll(c, step, 1), pltpu.roll(c, 128 - step, 1))

        def coefs(ref, h, r, n, step, scale, ins, cref, hc):
            lane = lax.broadcasted_iota(jnp.int32, (n + 16, 128), 1)
            c, (u, dn, l, rt, wl, wr) = shifts(ref, h, r, n, step)
            wl = jnp.where(lane < step, 0.0, wl)
            wr = jnp.where(lane >= 128 - step, 0.0, wr)
            t = 6.0 * c + u + dn + l + rt + wl + wr
            inv = jnp.where(ins[zone(r, n)] > 0.0, 1.0 / t, 0.0)
            cref[0, r + hc] = (c + u) * inv
            cref[1, r + hc] = (c + dn) * inv
            cref[2, r + hc] = (c + l) * inv
            cref[3, r + hc] = (c + rt) * inv
            cref[4, r + hc] = jnp.where(lane < step, 0.0, (c + wl) * inv)
            cref[5, r + hc] = jnp.where(lane >= 128 - step, 0.0, (c + wr) * inv)
            return t * (0.5 * scale), inv * (2.0 / scale)

        def update(ref, h, r, n, step, cref, hc, g):
            c, nb = shifts(ref, h, r, n, step)
            t = (g + cref[0, r + hc] * nb[0]) + cref[1, r + hc] * nb[1]
            s = cref[2, r + hc] * nb[2] + cref[3, r + hc] * nb[3]
            q = cref[4, r + hc] * nb[4] + cref[5, r + hc] * nb[5]
            return c, t + (s + q)

        def parity_of(n, step):
            return (lax.broadcasted_iota(jnp.int32, (n + 16, 128), 0)
                    + lax.broadcasted_iota(jnp.int32, (n + 16, 128), 1) // step) % 2

        def half(ref, h, n, step, cref, hc, g, colour, wide, masks=None):
            par = parity_of(n, step)
            ms = [par == colour, par == 1 - colour]
            for r in range(-wide, n + wide):
                c, new = update(ref, h, r, n, step, cref, hc, g(r))
                k = ms[r % 2]
                if masks is not None:
                    k = jnp.logical_and(k, masks[zone(r, n)])
                ref[r + h] = jnp.where(k, new, c)

        def fine(ref, colour, wide, masks=None):
            half(ref, H0, 16, 1, co, 4, lambda r: g0[r + 4], colour, wide, masks)

        def pairs(x, w):
            return x + jnp.where(lane8 % (2 * w) < w, pltpu.roll(x, 128 - w, 1), pltpu.roll(x, w, 1))

        ins0, ins1 = inside(16), inside(8)
        for r in range(16):
            e[r + H0, 8:24] = 1.0 + 0.5 * density[r]
            va[r + H0, 8:24] = previous[r]
            ch[r + H0, 8:24] = charge[r]
        for q in range(8):
            tmp[q, 0:16] = e[2 * q + H0, 8:24] + e[2 * q + 1 + H0, 8:24]
        for q in range(8):
            t = tmp[q, pl.ds(0, 8, stride=2), :] + tmp[q, pl.ds(1, 8, stride=2), :]
            e1[q + H1, 8:16] = pairs(t, 1) * 0.125
        send(4)

        recv(0)
        for r in range(-5, 21):
            z = zone(r, 16)
            for c0 in ((0, 24) if z == 1 else (0, 8, 16, 24)):
                e[r + H0, c0:c0 + 8] = ins0[z][c0:c0 + 8] * (1.0 + 0.5 * de[r + H0, c0:c0 + 8])
        recv(2)
        for r in range(-4, 20):
            dd, hh = coefs(e, H0, r, 16, 1, 1.0, ins0, co, 4)
            g0[r + 4] = ch[r + H0] * hh
            if 0 <= r < 16:
                d0[r] = dd[8:24]
        recv(1)
        for i in range(2 * NU):
            fine(va, i % 2, 3 - i)
        send(5)
        for r in range(16):
            vb[r + H0, 8:24] = va[r + H0, 8:24]
        recv(4)
        for r in range(-5, 13):
            dd, hh = coefs(e1, H1, r, 8, 2, 0.25, ins1, co1, 5)
            h1[r + 5] = hh
            if 0 <= r < 8:
                d1[r] = dd[8:16]
        recv(3)
        band = []
        for trio in ((4, 0, 6), (2, 8, 3), (7, 1, 5)):
            a, b, c = (lv[t] for t in trio)
            band.append(jnp.concatenate([a, b, b, c], axis=0))
        recv(5)
        for i in range(2 * EXTRA):
            if i % 2 == 0:
                masks = [x > i // 2 for x in band]
            fine(vb, i % 2, 4 - i, masks)
        for q in range(8):
            rs = []
            for r in (2 * q, 2 * q + 1):
                c, new = update(vb, H0, r, 16, 1, co, 4, g0[r + 4])
                rs.append(d0[r] * (new - c)[8:24])
            tmp[q, 0:16] = rs[0] + rs[1]
        for q in range(8):
            t = tmp[q, pl.ds(0, 8, stride=2), :] + tmp[q, pl.ds(1, 8, stride=2), :]
            s1[q + H1, 8:16] = pairs(t, 1) * 0.125
        send(6)
        send(7)
        recv(6)
        par = parity_of(8, 2)
        for r in range(-5, 13):
            h1[r + 5] = h1[r + 5] * s1[r + H1]
        for r in range(-4, 12):
            m[r + H1] = jnp.where(par == r % 2, h1[r + 5], 0.0)

        def middle(ref, colour, wide):
            half(ref, H1, 8, 2, co1, 5, lambda r: h1[r + 5], colour, wide)

        for i in range(1, 2 * NU):
            middle(m, i % 2, 4 - i)
        for q in range(4):
            rs = []
            for r in (2 * q, 2 * q + 1):
                c, new = update(m, H1, r, 8, 2, co1, 5, h1[r + 5])
                rs.append(d1[r] * (new - c)[8:16])
            tmp[q, 0:8] = pairs(rs[0] + rs[1], 2)
            tmp[q, 8:16] = pairs(e1[2 * q + H1, 8:16] + e1[2 * q + 1 + H1, 8:16], 2)
        lane1 = lax.broadcasted_iota(jnp.int32, (1, 128), 1)
        for k in range(2):
            for q in range(4):
                p = jnp.zeros((1, 128), jnp.float32)
                for j in range(4):
                    a = 8 * k + 2 * j
                    p = jnp.where(lane1 % 4 == j, tmp[q, a:a + 1] + tmp[q, a + 1:a + 2], p)
                gat[me, pl.ds(4 * k + q, 1)] = p * 0.125

        def gcopy(i):
            return pltpu.make_async_remote_copy(
                src_ref=gat.at[me], dst_ref=gat.at[me], send_sem=gsend, recv_sem=grecv,
                device_id=(i // nax, i % nax), device_id_type=MESH)

        def scatter(i, c):
            @pl.when(i != me)
            def _():
                gcopy(i).start()
            return c

        lax.fori_loop(0, nd, scatter, 0)
        send(8)
        everyone = pltpu.make_async_remote_copy(
            src_ref=gat.at[pl.ds(0, nd - 1)], dst_ref=gat.at[pl.ds(0, nd - 1)], send_sem=gsend, recv_sem=grecv,
            device_id=(ri, ai), device_id_type=MESH)
        everyone.wait_recv()

        n2 = nrad * 4
        zc = jnp.zeros((nax, 128), jnp.float32)
        sub = lax.broadcasted_iota(jnp.int32, (nax, 128), 0)
        lane = lax.broadcasted_iota(jnp.int32, (nax, 128), 1)
        j4 = lane % 4

        def around(c):
            lf = jnp.where(j4 == 0, pltpu.roll(pltpu.roll(c, 125, 1), 1, 0), pltpu.roll(c, 1, 1))
            rt = jnp.where(j4 == 3, pltpu.roll(pltpu.roll(c, 3, 1), nax - 1, 0), pltpu.roll(c, 127, 1))
            return lf, rt, pltpu.roll(c, 4, 1), pltpu.roll(c, 124, 1)

        first = jnp.logical_and(sub == 0, j4 == 0)
        last = jnp.logical_and(sub == nax - 1, j4 == 3)
        low = lane < 4
        high = lane >= 124
        eg[0] = zc
        eg[n2 + 1] = zc
        for r in range(n2 + 2 * PAD):
            f2[r] = zc
        for r in range(n2):
            eg[r + 1] = gat[(r // 4) * nax:(r // 4 + 1) * nax, 4 + r % 4, :]

        def coarse_coefs(r, _):
            c = eg[r + 1]
            lf, rt, wl, wr = around(c)
            lf = jnp.where(first, 0.0, lf)
            rt = jnp.where(last, 0.0, rt)
            wl = jnp.where(low, 0.0, wl)
            wr = jnp.where(high, 0.0, wr)
            u, dn = eg[r], eg[r + 2]
            t = 6.0 * c + u + dn + lf + rt + wl + wr
            h = 1.0 / t
            cg[0, r] = (c + u) * h
            cg[1, r] = (c + dn) * h
            cg[2, r] = jnp.where(first, 0.0, (c + lf) * h)
            cg[3, r] = jnp.where(last, 0.0, (c + rt) * h)
            cg[4, r] = jnp.where(low, 0.0, (c + wl) * h)
            cg[5, r] = jnp.where(high, 0.0, (c + wr) * h)
            sg[r] = h * 32.0
            return 0

        for r in range(n2):
            coarse_coefs(r, 0)
            sg[r] = sg[r] * gat[(r // 4) * nax:(r // 4 + 1) * nax, r % 4, :]
        par2 = (j4 + lane // 4) % 2

        def coarse_sweep(k, _):
            for colour in range(2):
                for r in range(n2):
                    c = f2[r + PAD]
                    lf, rt, wl, wr = around(c)
                    t = sg[r] + cg[0, r] * f2[r + PAD - 1] + cg[1, r] * f2[r + PAD + 1]
                    t = t + (cg[2, r] * lf + cg[3, r] * rt) + (cg[4, r] * wl + cg[5, r] * wr)
                    f2[r + PAD] = jnp.where(par2 == (colour + r) % 2, t, c)
            return 0

        lax.fori_loop(0, CS, coarse_sweep, 0)

        recv(8)
        m4 = lane8 % 4
        sides = ((jnp.maximum(ai - 1, 0), lo_a), (ai, None), (jnp.minimum(ai + 1, nax - 1), hi_a))
        for q in range(-3, 7):
            parts = []
            for at, ok in sides:
                own = jnp.broadcast_to(f2[4 * ri + q + PAD, pl.ds(at, 1), :], (8, 128))
                if ok is not None:
                    own = own * ok.astype(jnp.float32)
                t = jnp.zeros((8, 128), jnp.float32)
                want = sub8 // 2 - m4
                for s in range(-3, 4):
                    t = jnp.where(want == s, own if s == 0 else pltpu.roll(own, (-s) % 128, 1), t)
                parts.append(t)
            for r in (2 * q, 2 * q + 1):
                if 0 <= r < 8:
                    m2[r + H1, 0:8] = m2[r + H1, 0:8] + parts[0]
                    m2[r + H1, 8:16] = m[r + H1, 8:16] + parts[1]
                    m2[r + H1, 16:24] = m2[r + H1, 16:24] + parts[2]
                else:
                    for k in range(3):
                        m2[r + H1, 8 * k:8 * k + 8] = m2[r + H1, 8 * k:8 * k + 8] + parts[k]
        for i in range(2 * NU):
            middle(m2, i % 2, 5 - i)
        recv(7)
        for q in range(-2, 10):
            y = m2[q + H1]
            tmp[q + 2, pl.ds(0, 24, stride=2), :] = y
            tmp[q + 2, pl.ds(1, 24, stride=2), :] = y
        for r in range(-4, 20):
            t = tmp[r // 2 + 2, 8:40]
            if 0 <= r < 16:
                vc[r + H0, 0:8] = vc[r + H0, 0:8] + t[0:8]
                vc[r + H0, 8:24] = vb[r + H0, 8:24] + t[8:24]
                vc[r + H0, 24:32] = vc[r + H0, 24:32] + t[24:32]
            else:
                vc[r + H0] = vc[r + H0] + t
        for i in range(2 * NU):
            fine(vc, i % 2, 3 - i)
        out[...] = vc[H0:H0 + 16, 8:24]
        for d in range(8):
            @pl.when(has[d])
            def _(d=d):
                for x in range(NX):
                    copy(x, d, OPP[d]).wait_send()
        everyone.wait_send()

    return kernel


def solution(mesh):
    nrad, nax = mesh.shape["rad"], mesh.shape["ax"]
    nd = nrad * nax
    n2 = nrad * 4
    f32 = jnp.float32

    def on_device(charge, density, previous, levels):
        vm = pl.BlockSpec(memory_space=pltpu.VMEM)
        fine = pltpu.VMEM((16 + 2 * H0, 32, 128), f32)
        mid = pltpu.VMEM((8 + 2 * H1, 24, 128), f32)
        return pl.pallas_call(
            make_kernel(nrad, nax),
            out_shape=jax.ShapeDtypeStruct(charge.shape, f32),
            in_specs=[vm, vm, vm, pl.BlockSpec(memory_space=pltpu.SMEM)],
            out_specs=vm,
            scratch_shapes=[
                fine, fine, fine, fine, fine, fine,
                pltpu.VMEM((6, 24, 32, 128), f32),
                pltpu.VMEM((24, 32, 128), f32),
                pltpu.VMEM((16, 16, 128), f32),
                pltpu.VMEM((12, 48, 128), f32),
                pltpu.VMEM((9, 8, 128), jnp.int32),
                mid, mid, mid, mid,
                pltpu.VMEM((6, 18, 24, 128), f32),
                pltpu.VMEM((18, 24, 128), f32),
                pltpu.VMEM((8, 8, 128), f32),
                pltpu.VMEM((nd, 8, 128), f32),
                pltpu.VMEM((n2 + 2, nax, 128), f32),
                pltpu.VMEM((6, n2, nax, 128), f32),
                pltpu.VMEM((n2, nax, 128), f32),
                pltpu.VMEM((n2 + 2 * PAD, nax, 128), f32),
                pltpu.SemaphoreType.DMA((NX, 8)),
                pltpu.SemaphoreType.DMA((NX, 8)),
                pltpu.SemaphoreType.DMA,
                pltpu.SemaphoreType.DMA,
            ],
            compiler_params=pltpu.CompilerParams(
                collective_id=0, has_side_effects=True, vmem_limit_bytes=40 * 2**20),
        )(charge, density, previous, levels)

    return jax.shard_map(
        on_device, mesh=mesh,
        in_specs=(P("rad", "ax", None),) * 4,
        out_specs=P("rad", "ax", None), check_vma=False)
```

```python
import jax
import jax.numpy as jnp
from jax import lax
from jax.experimental import pallas as pl
from jax.experimental.pallas import tpu as pltpu
from jax.sharding import PartitionSpec as P

NU = 2
EXTRA = 2
CS = 8
PATCH = 16
MESH = pl.DeviceIdType.MESH
NX = 9
DIRS = ((-1, 0), (1, 0), (0, -1), (0, 1), (-1, -1), (1, 1), (-1, 1), (1, -1))
OPP = (1, 0, 3, 2, 5, 4, 7, 6)
H0 = 5
H1 = 6
PAD = 4


def make_kernel(nrad, nax):
    nd = nrad * nax

    def kernel(charge, density, previous, levels, out,
               de, e, ch, va, vb, vc, co, g0, d0, tmp, lv, e1, s1, m, m2, co1, h1, d1,
               pv, pt, pe, ps, pm, ssd, rsd, gat, eg, cg, sg, f2, send_sem, recv_sem, gsend, grecv):
        ri, ai = lax.axis_index("rad"), lax.axis_index("ax")
        me = ri * nax + ai
        lo_r, hi_r, lo_a, hi_a = ri > 0, ri < nrad - 1, ai > 0, ai < nax - 1
        okr = {-1: lo_r, 1: hi_r, 0: None}
        oka = {-1: lo_a, 1: hi_a, 0: None}
        has = []
        for dr, da in DIRS:
            x, y = okr[dr], oka[da]
            has.append(y if x is None else x if y is None else jnp.logical_and(x, y))

        barrier = pltpu.get_barrier_semaphore()

        def greet(i, c):
            @pl.when(i != me)
            def _():
                pl.semaphore_signal(barrier, inc=1, device_id=(i // nax, i % nax), device_id_type=MESH)
            return c

        lax.fori_loop(0, nd, greet, 0)

        plan = {
            0: (density, (0, 0), de, H0, 16, 16, 5),
            1: (pv, (0, 0), pt, 2, 8, 16, 2),
            2: (charge, (0, 0), ch, H0, 16, 16, 4),
            4: (pe, (3, 8), pe, 3, 4, 8, 3),
            5: (va, (H0, 8), vb, H0, 16, 16, 5),
            6: (ps, (3, 8), ps, 3, 4, 8, 3),
            7: (vb, (H0, 8), vc, H0, 16, 16, 4),
            8: (pm, (3, 8), pm, 3, 4, 8, 3),
        }
        side = {1: (0, 1, 4, 1), 2: (1, 2, 8, 2), 7: (2, 2, 8, 2)}

        def dest(x, d):
            dr, da = DIRS[d]
            if x == 3:
                return lv.at[d]
            if x in side and da:
                t, h, n, k = side[x]
                rows = {-1: (h - k, k), 0: (h, n), 1: (h + n, k)}[dr]
                return rsd.at[t, (da + 1) // 2, pl.ds(*rows)]
            tile, h, n, w, k = plan[x][2:]
            rows = {-1: (h - k, k), 0: (h, n), 1: (h + n, k)}[dr]
            cols = {-1: (0, 8), 0: (8, w), 1: (8 + w, 8)}[da]
            return tile.at[pl.ds(*rows), pl.ds(*cols)]

        def origin(x, d):
            dr, da = DIRS[d]
            if x == 3:
                return lv.at[8]
            if x in side and da:
                t, h, n, k = side[x]
                rows = {-1: (0, k), 0: (0, n), 1: (n - k, k)}[dr]
                return ssd.at[t, (da + 1) // 2, pl.ds(*rows)]
            src, off, _tile, h, n, w, k = plan[x]
            rows = {-1: (off[0], k), 0: (off[0], n), 1: (off[0] + n - k, k)}[dr]
            cols = {-1: (off[1], 8), 0: (off[1], w), 1: (off[1] + w - 8, 8)}[da]
            return src.at[pl.ds(*rows), pl.ds(*cols)]

        def copy(x, d, src, dst, slot):
            dr, da = DIRS[d]
            return pltpu.make_async_remote_copy(
                src_ref=src, dst_ref=dst, send_sem=send_sem.at[x, d], recv_sem=recv_sem.at[x, slot],
                device_id=(ri + dr, ai + da), device_id_type=MESH)

        def send(x):
            for d in range(8):
                @pl.when(has[d])
                def _(d=d):
                    copy(x, d, origin(x, d), dest(x, OPP[d]), OPP[d]).start()

        def recv(x):
            for d in range(8):
                @pl.when(has[d])
                def _(d=d):
                    copy(x, d, dest(x, d), dest(x, d), d).wait_recv()

        for d in range(8):
            @pl.when(jnp.logical_not(has[d]))
            def _(d=d):
                for x in range(NX):
                    ref = dest(x, d)
                    ref[...] = jnp.zeros(ref.shape, ref.dtype)

        lane8 = lax.broadcasted_iota(jnp.int32, (8, 128), 1)
        sub8 = lax.broadcasted_iota(jnp.int32, (8, 128), 0)
        lev = jnp.zeros((8, 128), jnp.int32)
        for p in range(8):
            lev = jnp.where(lane8 // PATCH == p, levels[0, 0, p], lev)
        lv[8] = lev

        def pack_sides(x, get):
            t, h, n, k = side[x]
            for q in range(n):
                a, b = get(2 * q), get(2 * q + 1)
                ssd[t, 0, q] = jnp.where(sub8 < 4, a[0:8], pltpu.roll(b[0:8], 4, 0))
                ssd[t, 1, q] = jnp.where(sub8 < 4, pltpu.roll(a[8:16], 4, 0), b[8:16])

        def unpack_sides(x, ref, off):
            t, h, n, k = side[x]
            for q in range(-k, n + k):
                a, b = rsd[t, 0, q + h], rsd[t, 1, q + h]
                ref[2 * q + off, 0:8] = pltpu.roll(a, 4, 0)
                ref[2 * q + 1 + off, 0:8] = a
                ref[2 * q + off, 24:32] = b
                ref[2 * q + 1 + off, 24:32] = pltpu.roll(b, 4, 0)

        def pack_rows(ref, q, a, b):
            ref[q + 3, 8:16] = jnp.where(lane8 % 2 == 0, a, b)

        lane24 = lax.broadcasted_iota(jnp.int32, (24, 128), 1)

        def unpack_rows(ref, dst):
            for q in range(-3, 7):
                p = ref[q + 3]
                dst[2 * q + H1] = jnp.where(lane24 % 2 == 0, p, pltpu.roll(p, 1, 1))
                dst[2 * q + 1 + H1] = jnp.where(lane24 % 2 == 0, pltpu.roll(p, 127, 1), p)

        odd16 = (lax.broadcasted_iota(jnp.int32, (16, 128), 0) + lax.broadcasted_iota(jnp.int32, (16, 128), 1)) % 2 == 1
        for q in range(8):
            p = jnp.where(odd16, previous[2 * q], previous[2 * q + 1])
            pv[q] = p
            pt[q + 2, 8:24] = p
        pack_sides(1, lambda q: pv[q])
        pack_sides(2, lambda r: charge[r])
        pl.semaphore_wait(barrier, nd - 1)
        send(0)
        send(2)
        send(1)
        send(3)

        def inside(n):
            sub = lax.broadcasted_iota(jnp.int32, (n + 16, 128), 0)
            left, right = lo_a.astype(jnp.float32), hi_a.astype(jnp.float32)
            row = jnp.where(sub < 8, left, jnp.where(sub >= n + 8, right, 1.0))
            return [row * lo_r.astype(jnp.float32), row, row * hi_r.astype(jnp.float32)]

        def zone(r, n):
            return 0 if r < 0 else 2 if r >= n else 1

        def shifts(ref, h, r, n, step):
            c = ref[r + h]
            return c, (ref[r + h - 1], ref[r + h + 1], pltpu.roll(c, 1, 0), pltpu.roll(c, n + 15, 0),
                       pltpu.roll(c, step, 1), pltpu.roll(c, 128 - step, 1))

        def coefs(ref, h, r, n, step, scale, ins, cref, hc):
            lane = lax.broadcasted_iota(jnp.int32, (n + 16, 128), 1)
            c, (u, dn, l, rt, wl, wr) = shifts(ref, h, r, n, step)
            wl = jnp.where(lane < step, 0.0, wl)
            wr = jnp.where(lane >= 128 - step, 0.0, wr)
            t = 6.0 * c + u + dn + l + rt + wl + wr
            inv = jnp.where(ins[zone(r, n)] > 0.0, 1.0 / t, 0.0)
            cref[0, r + hc] = (c + u) * inv
            cref[1, r + hc] = (c + dn) * inv
            cref[2, r + hc] = (c + l) * inv
            cref[3, r + hc] = (c + rt) * inv
            cref[4, r + hc] = jnp.where(lane < step, 0.0, (c + wl) * inv)
            cref[5, r + hc] = jnp.where(lane >= 128 - step, 0.0, (c + wr) * inv)
            return t * (0.5 * scale), inv * (2.0 / scale)

        def update(ref, h, r, n, step, cref, hc, g):
            c, nb = shifts(ref, h, r, n, step)
            t = (g + cref[0, r + hc] * nb[0]) + cref[1, r + hc] * nb[1]
            s = cref[2, r + hc] * nb[2] + cref[3, r + hc] * nb[3]
            q = cref[4, r + hc] * nb[4] + cref[5, r + hc] * nb[5]
            return c, t + (s + q)

        def parity_of(n, step):
            return (lax.broadcasted_iota(jnp.int32, (n + 16, 128), 0)
                    + lax.broadcasted_iota(jnp.int32, (n + 16, 128), 1) // step) % 2

        def half(ref, h, n, step, cref, hc, g, colour, wide, masks=None):
            par = parity_of(n, step)
            ms = [par == colour, par == 1 - colour]
            for r in range(-wide, n + wide):
                c, new = update(ref, h, r, n, step, cref, hc, g(r))
                k = ms[r % 2]
                if masks is not None:
                    k = jnp.logical_and(k, masks[zone(r, n)])
                ref[r + h] = jnp.where(k, new, c)

        def fine(ref, colour, wide, masks=None):
            half(ref, H0, 16, 1, co, 4, lambda r: g0[r + 4], colour, wide, masks)

        def pairs(x, w):
            return x + jnp.where(lane8 % (2 * w) < w, pltpu.roll(x, 128 - w, 1), pltpu.roll(x, w, 1))

        ins0, ins1 = inside(16), inside(8)
        for r in range(16):
            e[r + H0, 8:24] = 1.0 + 0.5 * density[r]
            ch[r + H0, 8:24] = charge[r]
        for q in range(8):
            tmp[q, 0:16] = e[2 * q + H0, 8:24] + e[2 * q + 1 + H0, 8:24]
        for q in range(4):
            t = [tmp[p, pl.ds(0, 8, stride=2), :] + tmp[p, pl.ds(1, 8, stride=2), :] for p in (2 * q, 2 * q + 1)]
            pack_rows(pe, q, pairs(t[0], 1) * 0.125, pairs(t[1], 1) * 0.125)

        recv(0)
        for r in range(-5, 21):
            z = zone(r, 16)
            for c0 in ((0, 24) if z == 1 else (0, 8, 16, 24)):
                e[r + H0, c0:c0 + 8] = ins0[z][c0:c0 + 8] * (1.0 + 0.5 * de[r + H0, c0:c0 + 8])
        recv(2)
        unpack_sides(2, ch, H0)
        for r in range(-4, 20):
            dd, hh = coefs(e, H0, r, 16, 1, 1.0, ins0, co, 4)
            g0[r + 4] = ch[r + H0] * hh
            if 0 <= r < 16:
                d0[r] = dd[8:24]
        recv(1)
        send(4)
        unpack_sides(1, pt, 2)
        for q in range(-2, 10):
            va[2 * q + H0] = pt[q + 2]
            va[2 * q + 1 + H0] = pt[q + 2]
        for i in range(2 * NU):
            fine(va, i % 2, 3 - i)
        send(5)
        for r in range(16):
            vb[r + H0, 8:24] = va[r + H0, 8:24]
        recv(4)
        unpack_rows(pe, e1)
        for r in range(-5, 13):
            dd, hh = coefs(e1, H1, r, 8, 2, 0.25, ins1, co1, 5)
            h1[r + 5] = hh
            if 0 <= r < 8:
                d1[r] = dd[8:16]
        recv(3)
        band = []
        for trio in ((4, 0, 6), (2, 8, 3), (7, 1, 5)):
            a, b, c = (lv[t] for t in trio)
            band.append(jnp.concatenate([a, b, b, c], axis=0))
        recv(5)
        for i in range(2 * EXTRA):
            if i % 2 == 0:
                masks = [x > i // 2 for x in band]
            fine(vb, i % 2, 4 - i, masks)
        for q in range(8):
            rs = []
            for r in (2 * q, 2 * q + 1):
                c, new = update(vb, H0, r, 16, 1, co, 4, g0[r + 4])
                rs.append(d0[r] * (new - c)[8:24])
            tmp[q, 0:16] = rs[0] + rs[1]
        for q in range(4):
            t = [tmp[p, pl.ds(0, 8, stride=2), :] + tmp[p, pl.ds(1, 8, stride=2), :] for p in (2 * q, 2 * q + 1)]
            pack_rows(ps, q, pairs(t[0], 1) * 0.125, pairs(t[1], 1) * 0.125)
        send(6)
        pack_sides(7, lambda r: vb[r + H0, 8:24])
        recv(6)
        send(7)
        unpack_rows(ps, s1)
        par = parity_of(8, 2)
        for r in range(-5, 13):
            h1[r + 5] = h1[r + 5] * s1[r + H1]
        for r in range(-4, 12):
            m[r + H1] = jnp.where(par == r % 2, h1[r + 5], 0.0)

        def middle(ref, colour, wide):
            half(ref, H1, 8, 2, co1, 5, lambda r: h1[r + 5], colour, wide)

        for i in range(1, 2 * NU):
            middle(m, i % 2, 4 - i)
        for q in range(4):
            rs = []
            for r in (2 * q, 2 * q + 1):
                c, new = update(m, H1, r, 8, 2, co1, 5, h1[r + 5])
                rs.append(d1[r] * (new - c)[8:16])
            tmp[q, 0:8] = pairs(rs[0] + rs[1], 2)
            tmp[q, 8:16] = pairs(e1[2 * q + H1, 8:16] + e1[2 * q + 1 + H1, 8:16], 2)
        lane1 = lax.broadcasted_iota(jnp.int32, (1, 128), 1)
        for k in range(2):
            for q in range(4):
                p = jnp.zeros((1, 128), jnp.float32)
                for j in range(4):
                    a = 8 * k + 2 * j
                    p = jnp.where(lane1 % 4 == j, tmp[q, a:a + 1] + tmp[q, a + 1:a + 2], p)
                gat[me, pl.ds(4 * k + q, 1)] = p * 0.125

        def gcopy(i):
            return pltpu.make_async_remote_copy(
                src_ref=gat.at[me], dst_ref=gat.at[me], send_sem=gsend, recv_sem=grecv,
                device_id=(i // nax, i % nax), device_id_type=MESH)

        def scatter(i, c):
            @pl.when(i != me)
            def _():
                gcopy(i).start()
            return c

        lax.fori_loop(0, nd, scatter, 0)
        for q in range(4):
            pack_rows(pm, q, m[2 * q + H1, 8:16], m[2 * q + 1 + H1, 8:16])
        send(8)
        everyone = pltpu.make_async_remote_copy(
            src_ref=gat.at[pl.ds(0, nd - 1)], dst_ref=gat.at[pl.ds(0, nd - 1)], send_sem=gsend, recv_sem=grecv,
            device_id=(ri, ai), device_id_type=MESH)
        everyone.wait_recv()

        n2 = nrad * 4
        zc = jnp.zeros((nax, 128), jnp.float32)
        sub = lax.broadcasted_iota(jnp.int32, (nax, 128), 0)
        lane = lax.broadcasted_iota(jnp.int32, (nax, 128), 1)
        j4 = lane % 4

        def around(c):
            lf = jnp.where(j4 == 0, pltpu.roll(pltpu.roll(c, 125, 1), 1, 0), pltpu.roll(c, 1, 1))
            rt = jnp.where(j4 == 3, pltpu.roll(pltpu.roll(c, 3, 1), nax - 1, 0), pltpu.roll(c, 127, 1))
            return lf, rt, pltpu.roll(c, 4, 1), pltpu.roll(c, 124, 1)

        first = jnp.logical_and(sub == 0, j4 == 0)
        last = jnp.logical_and(sub == nax - 1, j4 == 3)
        low = lane < 4
        high = lane >= 124
        eg[0] = zc
        eg[n2 + 1] = zc
        for r in range(n2 + 2 * PAD):
            f2[r] = zc
        for r in range(n2):
            eg[r + 1] = gat[(r // 4) * nax:(r // 4 + 1) * nax, 4 + r % 4, :]

        def coarse_coefs(r, _):
            c = eg[r + 1]
            lf, rt, wl, wr = around(c)
            lf = jnp.where(first, 0.0, lf)
            rt = jnp.where(last, 0.0, rt)
            wl = jnp.where(low, 0.0, wl)
            wr = jnp.where(high, 0.0, wr)
            u, dn = eg[r], eg[r + 2]
            t = 6.0 * c + u + dn + lf + rt + wl + wr
            h = 1.0 / t
            cg[0, r] = (c + u) * h
            cg[1, r] = (c + dn) * h
            cg[2, r] = jnp.where(first, 0.0, (c + lf) * h)
            cg[3, r] = jnp.where(last, 0.0, (c + rt) * h)
            cg[4, r] = jnp.where(low, 0.0, (c + wl) * h)
            cg[5, r] = jnp.where(high, 0.0, (c + wr) * h)
            sg[r] = h * 32.0
            return 0

        for r in range(n2):
            coarse_coefs(r, 0)
            sg[r] = sg[r] * gat[(r // 4) * nax:(r // 4 + 1) * nax, r % 4, :]
        par2 = (j4 + lane // 4) % 2

        def coarse_sweep(k, _):
            for colour in range(2):
                for r in range(n2):
                    c = f2[r + PAD]
                    lf, rt, wl, wr = around(c)
                    t = sg[r] + cg[0, r] * f2[r + PAD - 1] + cg[1, r] * f2[r + PAD + 1]
                    t = t + (cg[2, r] * lf + cg[3, r] * rt) + (cg[4, r] * wl + cg[5, r] * wr)
                    f2[r + PAD] = jnp.where(par2 == (colour + r) % 2, t, c)
            return 0

        lax.fori_loop(0, CS, coarse_sweep, 0)

        recv(8)
        unpack_rows(pm, m2)
        m4 = lane8 % 4
        sides = ((jnp.maximum(ai - 1, 0), lo_a), (ai, None), (jnp.minimum(ai + 1, nax - 1), hi_a))
        for q in range(-3, 7):
            parts = []
            for at, ok in sides:
                own = jnp.broadcast_to(f2[4 * ri + q + PAD, pl.ds(at, 1), :], (8, 128))
                if ok is not None:
                    own = own * ok.astype(jnp.float32)
                t = jnp.zeros((8, 128), jnp.float32)
                want = sub8 // 2 - m4
                for s in range(-3, 4):
                    t = jnp.where(want == s, own if s == 0 else pltpu.roll(own, (-s) % 128, 1), t)
                parts.append(t)
            for r in (2 * q, 2 * q + 1):
                for k in range(3):
                    m2[r + H1, 8 * k:8 * k + 8] = m2[r + H1, 8 * k:8 * k + 8] + parts[k]
        for i in range(2 * NU):
            middle(m2, i % 2, 5 - i)
        recv(7)
        unpack_sides(7, vc, H0)
        for q in range(-2, 10):
            y = m2[q + H1]
            tmp[q + 2, pl.ds(0, 24, stride=2), :] = y
            tmp[q + 2, pl.ds(1, 24, stride=2), :] = y
        for r in range(-4, 20):
            t = tmp[r // 2 + 2, 8:40]
            if 0 <= r < 16:
                vc[r + H0, 0:8] = vc[r + H0, 0:8] + t[0:8]
                vc[r + H0, 8:24] = vb[r + H0, 8:24] + t[8:24]
                vc[r + H0, 24:32] = vc[r + H0, 24:32] + t[24:32]
            else:
                vc[r + H0] = vc[r + H0] + t
        for i in range(2 * NU):
            fine(vc, i % 2, 3 - i)
        out[...] = vc[H0:H0 + 16, 8:24]
        for d in range(8):
            @pl.when(has[d])
            def _(d=d):
                for x in range(NX):
                    copy(x, d, origin(x, d), origin(x, d), OPP[d]).wait_send()
        everyone.wait_send()

    return kernel


def solution(mesh):
    nrad, nax = mesh.shape["rad"], mesh.shape["ax"]
    nd = nrad * nax
    n2 = nrad * 4
    f32 = jnp.float32

    def on_device(charge, density, previous, levels):
        vm = pl.BlockSpec(memory_space=pltpu.VMEM)
        fine = pltpu.VMEM((16 + 2 * H0, 32, 128), f32)
        mid = pltpu.VMEM((8 + 2 * H1, 24, 128), f32)
        pack = pltpu.VMEM((10, 24, 128), f32)
        return pl.pallas_call(
            make_kernel(nrad, nax),
            out_shape=jax.ShapeDtypeStruct(charge.shape, f32),
            in_specs=[vm, vm, vm, pl.BlockSpec(memory_space=pltpu.SMEM)],
            out_specs=vm,
            scratch_shapes=[
                fine, fine, fine, fine, fine, fine,
                pltpu.VMEM((6, 24, 32, 128), f32),
                pltpu.VMEM((24, 32, 128), f32),
                pltpu.VMEM((16, 16, 128), f32),
                pltpu.VMEM((12, 48, 128), f32),
                pltpu.VMEM((9, 8, 128), jnp.int32),
                mid, mid, mid, mid,
                pltpu.VMEM((6, 18, 24, 128), f32),
                pltpu.VMEM((18, 24, 128), f32),
                pltpu.VMEM((8, 8, 128), f32),
                pltpu.VMEM((8, 16, 128), f32),
                pltpu.VMEM((12, 32, 128), f32),
                pack, pack, pack,
                pltpu.VMEM((3, 2, 8, 8, 128), f32),
                pltpu.VMEM((3, 2, 12, 8, 128), f32),
                pltpu.VMEM((nd, 8, 128), f32),
                pltpu.VMEM((n2 + 2, nax, 128), f32),
                pltpu.VMEM((6, n2, nax, 128), f32),
                pltpu.VMEM((n2, nax, 128), f32),
                pltpu.VMEM((n2 + 2 * PAD, nax, 128), f32),
                pltpu.SemaphoreType.DMA((NX, 8)),
                pltpu.SemaphoreType.DMA((NX, 8)),
                pltpu.SemaphoreType.DMA,
                pltpu.SemaphoreType.DMA,
            ],
            compiler_params=pltpu.CompilerParams(
                collective_id=0, has_side_effects=True, vmem_limit_bytes=40 * 2**20),
        )(charge, density, previous, levels)

    return jax.shard_map(
        on_device, mesh=mesh,
        in_specs=(P("rad", "ax", None),) * 4,
        out_specs=P("rad", "ax", None), check_vma=False)
```

```python
import jax
import jax.numpy as jnp
from jax import lax
from jax.experimental import pallas as pl
from jax.experimental.pallas import tpu as pltpu
from jax.sharding import PartitionSpec as P

NU = 2
EXTRA = 2
CS = 8
PATCH = 16
MESH = pl.DeviceIdType.MESH
NX = 9
DIRS = ((-1, 0), (1, 0), (0, -1), (0, 1), (-1, -1), (1, 1), (-1, 1), (1, -1))
OPP = (1, 0, 3, 2, 5, 4, 7, 6)
H0 = 5
H1 = 6
PAD = 4


def make_kernel(nrad, nax):
    nd = nrad * nax

    def kernel(charge_in, density_in, previous_in, levels_in, out, charge, density, previous, levels, lsem,
               de, e, ch, va, vb, vc, co, g0, d0, tmp, lv, e1, s1, m, m2, co1, h1, d1,
               pv, pt, pe, ps, pm, ssd, rsd, gat, eg, cg, sg, f2, send_sem, recv_sem, gsend, grecv):
        ri, ai = lax.axis_index("rad"), lax.axis_index("ax")
        me = ri * nax + ai
        lo_r, hi_r, lo_a, hi_a = ri > 0, ri < nrad - 1, ai > 0, ai < nax - 1
        okr = {-1: lo_r, 1: hi_r, 0: None}
        oka = {-1: lo_a, 1: hi_a, 0: None}
        has = []
        for dr, da in DIRS:
            x, y = okr[dr], oka[da]
            has.append(y if x is None else x if y is None else jnp.logical_and(x, y))

        loads = [pltpu.make_async_copy(a, b, lsem.at[i]) for i, (a, b) in enumerate((
            (previous_in, previous), (charge_in, charge), (density_in, density), (levels_in, levels)))]
        for c in loads:
            c.start()
        barrier = pltpu.get_barrier_semaphore()

        def greet(i, c):
            @pl.when(i != me)
            def _():
                pl.semaphore_signal(barrier, inc=1, device_id=(i // nax, i % nax), device_id_type=MESH)
            return c

        lax.fori_loop(0, nd, greet, 0)

        plan = {
            0: (density, (0, 0), de, H0, 16, 16, 5),
            1: (pv, (0, 0), pt, 2, 8, 16, 2),
            2: (charge, (0, 0), ch, H0, 16, 16, 4),
            4: (pe, (3, 8), pe, 3, 4, 8, 3),
            5: (va, (H0, 8), vb, H0, 16, 16, 5),
            6: (ps, (3, 8), ps, 3, 4, 8, 3),
            7: (vb, (H0, 8), vc, H0, 16, 16, 4),
            8: (pm, (3, 8), pm, 3, 4, 8, 3),
        }
        side = {1: (0, 1, 4, 1), 2: (1, 2, 8, 2), 7: (2, 2, 8, 2)}

        def dest(x, d):
            dr, da = DIRS[d]
            if x == 3:
                return lv.at[d]
            if x in side and da:
                t, h, n, k = side[x]
                rows = {-1: (h - k, k), 0: (h, n), 1: (h + n, k)}[dr]
                return rsd.at[t, (da + 1) // 2, pl.ds(*rows)]
            tile, h, n, w, k = plan[x][2:]
            rows = {-1: (h - k, k), 0: (h, n), 1: (h + n, k)}[dr]
            cols = {-1: (0, 8), 0: (8, w), 1: (8 + w, 8)}[da]
            return tile.at[pl.ds(*rows), pl.ds(*cols)]

        def origin(x, d):
            dr, da = DIRS[d]
            if x == 3:
                return lv.at[8]
            if x in side and da:
                t, h, n, k = side[x]
                rows = {-1: (0, k), 0: (0, n), 1: (n - k, k)}[dr]
                return ssd.at[t, (da + 1) // 2, pl.ds(*rows)]
            src, off, _tile, h, n, w, k = plan[x]
            rows = {-1: (off[0], k), 0: (off[0], n), 1: (off[0] + n - k, k)}[dr]
            cols = {-1: (off[1], 8), 0: (off[1], w), 1: (off[1] + w - 8, 8)}[da]
            return src.at[pl.ds(*rows), pl.ds(*cols)]

        def copy(x, d, src, dst, slot):
            dr, da = DIRS[d]
            return pltpu.make_async_remote_copy(
                src_ref=src, dst_ref=dst, send_sem=send_sem.at[x, d], recv_sem=recv_sem.at[x, slot],
                device_id=(ri + dr, ai + da), device_id_type=MESH)

        def send(x):
            for d in range(8):
                @pl.when(has[d])
                def _(d=d):
                    copy(x, d, origin(x, d), dest(x, OPP[d]), OPP[d]).start()

        def recv(x):
            for d in range(8):
                @pl.when(has[d])
                def _(d=d):
                    copy(x, d, dest(x, d), dest(x, d), d).wait_recv()

        for d in range(8):
            @pl.when(jnp.logical_not(has[d]))
            def _(d=d):
                for x in range(NX):
                    ref = dest(x, d)
                    ref[...] = jnp.zeros(ref.shape, ref.dtype)

        for c in loads:
            c.wait()
        lane8 = lax.broadcasted_iota(jnp.int32, (8, 128), 1)
        sub8 = lax.broadcasted_iota(jnp.int32, (8, 128), 0)
        lev = jnp.zeros((8, 128), jnp.int32)
        for p in range(8):
            lev = jnp.where(lane8 // PATCH == p, levels[0, 0, p], lev)
        lv[8] = lev

        def pack_sides(x, get):
            t, h, n, k = side[x]
            for q in range(n):
                a, b = get(2 * q), get(2 * q + 1)
                ssd[t, 0, q] = jnp.where(sub8 < 4, a[0:8], pltpu.roll(b[0:8], 4, 0))
                ssd[t, 1, q] = jnp.where(sub8 < 4, pltpu.roll(a[8:16], 4, 0), b[8:16])

        def unpack_sides(x, ref, off):
            t, h, n, k = side[x]
            for q in range(-k, n + k):
                a, b = rsd[t, 0, q + h], rsd[t, 1, q + h]
                ref[2 * q + off, 0:8] = pltpu.roll(a, 4, 0)
                ref[2 * q + 1 + off, 0:8] = a
                ref[2 * q + off, 24:32] = b
                ref[2 * q + 1 + off, 24:32] = pltpu.roll(b, 4, 0)

        def pack_rows(ref, q, a, b):
            ref[q + 3, 8:16] = jnp.where(lane8 % 2 == 0, a, b)

        lane24 = lax.broadcasted_iota(jnp.int32, (24, 128), 1)

        def unpack_rows(ref, dst):
            for q in range(-3, 7):
                p = ref[q + 3]
                dst[2 * q + H1] = jnp.where(lane24 % 2 == 0, p, pltpu.roll(p, 1, 1))
                dst[2 * q + 1 + H1] = jnp.where(lane24 % 2 == 0, pltpu.roll(p, 127, 1), p)

        odd16 = (lax.broadcasted_iota(jnp.int32, (16, 128), 0) + lax.broadcasted_iota(jnp.int32, (16, 128), 1)) % 2 == 1
        for q in range(8):
            p = jnp.where(odd16, previous[2 * q], previous[2 * q + 1])
            pv[q] = p
            pt[q + 2, 8:24] = p
        pack_sides(1, lambda q: pv[q])
        pack_sides(2, lambda r: charge[r])
        pl.semaphore_wait(barrier, nd - 1)
        send(0)
        send(2)
        send(1)
        send(3)

        def inside(n):
            sub = lax.broadcasted_iota(jnp.int32, (n + 16, 128), 0)
            left, right = lo_a.astype(jnp.float32), hi_a.astype(jnp.float32)
            row = jnp.where(sub < 8, left, jnp.where(sub >= n + 8, right, 1.0))
            return [row * lo_r.astype(jnp.float32), row, row * hi_r.astype(jnp.float32)]

        def zone(r, n):
            return 0 if r < 0 else 2 if r >= n else 1

        def shifts(ref, h, r, n, step):
            c = ref[r + h]
            return c, (ref[r + h - 1], ref[r + h + 1], pltpu.roll(c, 1, 0), pltpu.roll(c, n + 15, 0),
                       pltpu.roll(c, step, 1), pltpu.roll(c, 128 - step, 1))

        def coefs(ref, h, r, n, step, scale, ins, cref, hc):
            lane = lax.broadcasted_iota(jnp.int32, (n + 16, 128), 1)
            c, (u, dn, l, rt, wl, wr) = shifts(ref, h, r, n, step)
            wl = jnp.where(lane < step, 0.0, wl)
            wr = jnp.where(lane >= 128 - step, 0.0, wr)
            t = 6.0 * c + u + dn + l + rt + wl + wr
            inv = jnp.where(ins[zone(r, n)] > 0.0, 1.0 / t, 0.0)
            cref[0, r + hc] = (c + u) * inv
            cref[1, r + hc] = (c + dn) * inv
            cref[2, r + hc] = (c + l) * inv
            cref[3, r + hc] = (c + rt) * inv
            cref[4, r + hc] = jnp.where(lane < step, 0.0, (c + wl) * inv)
            cref[5, r + hc] = jnp.where(lane >= 128 - step, 0.0, (c + wr) * inv)
            return t * (0.5 * scale), inv * (2.0 / scale)

        def update(ref, h, r, n, step, cref, hc, g):
            c, nb = shifts(ref, h, r, n, step)
            t = (g + cref[0, r + hc] * nb[0]) + cref[1, r + hc] * nb[1]
            s = cref[2, r + hc] * nb[2] + cref[3, r + hc] * nb[3]
            q = cref[4, r + hc] * nb[4] + cref[5, r + hc] * nb[5]
            return c, t + (s + q)

        def parity_of(n, step):
            return (lax.broadcasted_iota(jnp.int32, (n + 16, 128), 0)
                    + lax.broadcasted_iota(jnp.int32, (n + 16, 128), 1) // step) % 2

        def half(ref, h, n, step, cref, hc, g, colour, wide, masks=None):
            par = parity_of(n, step)
            ms = [par == colour, par == 1 - colour]
            for r in range(-wide, n + wide):
                c, new = update(ref, h, r, n, step, cref, hc, g(r))
                k = ms[r % 2]
                if masks is not None:
                    k = jnp.logical_and(k, masks[zone(r, n)])
                ref[r + h] = jnp.where(k, new, c)

        def fine(ref, colour, wide, masks=None):
            half(ref, H0, 16, 1, co, 4, lambda r: g0[r + 4], colour, wide, masks)

        def pairs(x, w):
            return x + jnp.where(lane8 % (2 * w) < w, pltpu.roll(x, 128 - w, 1), pltpu.roll(x, w, 1))

        ins0, ins1 = inside(16), inside(8)
        for r in range(16):
            e[r + H0, 8:24] = 1.0 + 0.5 * density[r]
            ch[r + H0, 8:24] = charge[r]
        for q in range(8):
            tmp[q, 0:16] = e[2 * q + H0, 8:24] + e[2 * q + 1 + H0, 8:24]
        for q in range(4):
            t = [tmp[p, pl.ds(0, 8, stride=2), :] + tmp[p, pl.ds(1, 8, stride=2), :] for p in (2 * q, 2 * q + 1)]
            pack_rows(pe, q, pairs(t[0], 1) * 0.125, pairs(t[1], 1) * 0.125)

        recv(0)
        for r in range(-5, 21):
            z = zone(r, 16)
            for c0 in ((0, 24) if z == 1 else (0, 8, 16, 24)):
                e[r + H0, c0:c0 + 8] = ins0[z][c0:c0 + 8] * (1.0 + 0.5 * de[r + H0, c0:c0 + 8])
        recv(2)
        unpack_sides(2, ch, H0)
        for r in range(-4, 20):
            dd, hh = coefs(e, H0, r, 16, 1, 1.0, ins0, co, 4)
            g0[r + 4] = ch[r + H0] * hh
            if 0 <= r < 16:
                d0[r] = dd[8:24]
        recv(1)
        send(4)
        unpack_sides(1, pt, 2)
        for q in range(-2, 10):
            va[2 * q + H0] = pt[q + 2]
            va[2 * q + 1 + H0] = pt[q + 2]
        for i in range(2 * NU):
            fine(va, i % 2, 3 - i)
        send(5)
        for r in range(16):
            vb[r + H0, 8:24] = va[r + H0, 8:24]
        recv(4)
        unpack_rows(pe, e1)
        for r in range(-5, 13):
            dd, hh = coefs(e1, H1, r, 8, 2, 0.25, ins1, co1, 5)
            h1[r + 5] = hh
            if 0 <= r < 8:
                d1[r] = dd[8:16]
        recv(3)
        band = []
        for trio in ((4, 0, 6), (2, 8, 3), (7, 1, 5)):
            a, b, c = (lv[t] for t in trio)
            band.append(jnp.concatenate([a, b, b, c], axis=0))
        recv(5)
        for i in range(2 * EXTRA):
            if i % 2 == 0:
                masks = [x > i // 2 for x in band]
            fine(vb, i % 2, 4 - i, masks)
        for q in range(8):
            rs = []
            for r in (2 * q, 2 * q + 1):
                c, new = update(vb, H0, r, 16, 1, co, 4, g0[r + 4])
                rs.append(d0[r] * (new - c)[8:24])
            tmp[q, 0:16] = rs[0] + rs[1]
        for q in range(4):
            t = [tmp[p, pl.ds(0, 8, stride=2), :] + tmp[p, pl.ds(1, 8, stride=2), :] for p in (2 * q, 2 * q + 1)]
            pack_rows(ps, q, pairs(t[0], 1) * 0.125, pairs(t[1], 1) * 0.125)
        send(6)
        pack_sides(7, lambda r: vb[r + H0, 8:24])
        recv(6)
        send(7)
        unpack_rows(ps, s1)
        par = parity_of(8, 2)
        for r in range(-5, 13):
            h1[r + 5] = h1[r + 5] * s1[r + H1]
        for r in range(-4, 12):
            m[r + H1] = jnp.where(par == r % 2, h1[r + 5], 0.0)

        def middle(ref, colour, wide):
            half(ref, H1, 8, 2, co1, 5, lambda r: h1[r + 5], colour, wide)

        for i in range(1, 2 * NU):
            middle(m, i % 2, 4 - i)
        for q in range(4):
            rs = []
            for r in (2 * q, 2 * q + 1):
                c, new = update(m, H1, r, 8, 2, co1, 5, h1[r + 5])
                rs.append(d1[r] * (new - c)[8:16])
            tmp[q, 0:8] = pairs(rs[0] + rs[1], 2)
            tmp[q, 8:16] = pairs(e1[2 * q + H1, 8:16] + e1[2 * q + 1 + H1, 8:16], 2)
        lane1 = lax.broadcasted_iota(jnp.int32, (1, 128), 1)
        for k in range(2):
            for q in range(4):
                p = jnp.zeros((1, 128), jnp.float32)
                for j in range(4):
                    a = 8 * k + 2 * j
                    p = jnp.where(lane1 % 4 == j, tmp[q, a:a + 1] + tmp[q, a + 1:a + 2], p)
                gat[me, pl.ds(4 * k + q, 1)] = p * 0.125

        def gcopy(i):
            return pltpu.make_async_remote_copy(
                src_ref=gat.at[me], dst_ref=gat.at[me], send_sem=gsend, recv_sem=grecv,
                device_id=(i // nax, i % nax), device_id_type=MESH)

        def scatter(i, c):
            @pl.when(i != me)
            def _():
                gcopy(i).start()
            return c

        lax.fori_loop(0, nd, scatter, 0)
        for q in range(4):
            pack_rows(pm, q, m[2 * q + H1, 8:16], m[2 * q + 1 + H1, 8:16])
        send(8)
        everyone = pltpu.make_async_remote_copy(
            src_ref=gat.at[pl.ds(0, nd - 1)], dst_ref=gat.at[pl.ds(0, nd - 1)], send_sem=gsend, recv_sem=grecv,
            device_id=(ri, ai), device_id_type=MESH)
        everyone.wait_recv()

        n2 = nrad * 4
        zc = jnp.zeros((nax, 128), jnp.float32)
        sub = lax.broadcasted_iota(jnp.int32, (nax, 128), 0)
        lane = lax.broadcasted_iota(jnp.int32, (nax, 128), 1)
        j4 = lane % 4

        def around(c):
            lf = jnp.where(j4 == 0, pltpu.roll(pltpu.roll(c, 125, 1), 1, 0), pltpu.roll(c, 1, 1))
            rt = jnp.where(j4 == 3, pltpu.roll(pltpu.roll(c, 3, 1), nax - 1, 0), pltpu.roll(c, 127, 1))
            return lf, rt, pltpu.roll(c, 4, 1), pltpu.roll(c, 124, 1)

        first = jnp.logical_and(sub == 0, j4 == 0)
        last = jnp.logical_and(sub == nax - 1, j4 == 3)
        low = lane < 4
        high = lane >= 124
        eg[0] = zc
        eg[n2 + 1] = zc
        for r in range(n2 + 2 * PAD):
            f2[r] = zc
        for r in range(n2):
            eg[r + 1] = gat[(r // 4) * nax:(r // 4 + 1) * nax, 4 + r % 4, :]

        def coarse_coefs(r, _):
            c = eg[r + 1]
            lf, rt, wl, wr = around(c)
            lf = jnp.where(first, 0.0, lf)
            rt = jnp.where(last, 0.0, rt)
            wl = jnp.where(low, 0.0, wl)
            wr = jnp.where(high, 0.0, wr)
            u, dn = eg[r], eg[r + 2]
            t = 6.0 * c + u + dn + lf + rt + wl + wr
            h = 1.0 / t
            cg[0, r] = (c + u) * h
            cg[1, r] = (c + dn) * h
            cg[2, r] = jnp.where(first, 0.0, (c + lf) * h)
            cg[3, r] = jnp.where(last, 0.0, (c + rt) * h)
            cg[4, r] = jnp.where(low, 0.0, (c + wl) * h)
            cg[5, r] = jnp.where(high, 0.0, (c + wr) * h)
            sg[r] = h * 32.0
            return 0

        for r in range(n2):
            coarse_coefs(r, 0)
            sg[r] = sg[r] * gat[(r // 4) * nax:(r // 4 + 1) * nax, r % 4, :]
        par2 = (j4 + lane // 4) % 2

        def coarse_sweep(k, _):
            for colour in range(2):
                for r in range(n2):
                    c = f2[r + PAD]
                    lf, rt, wl, wr = around(c)
                    t = sg[r] + cg[0, r] * f2[r + PAD - 1] + cg[1, r] * f2[r + PAD + 1]
                    t = t + (cg[2, r] * lf + cg[3, r] * rt) + (cg[4, r] * wl + cg[5, r] * wr)
                    f2[r + PAD] = jnp.where(par2 == (colour + r) % 2, t, c)
            return 0

        lax.fori_loop(0, CS, coarse_sweep, 0)

        recv(8)
        unpack_rows(pm, m2)
        m4 = lane8 % 4
        sides = ((jnp.maximum(ai - 1, 0), lo_a), (ai, None), (jnp.minimum(ai + 1, nax - 1), hi_a))
        for q in range(-3, 7):
            parts = []
            for at, ok in sides:
                own = jnp.broadcast_to(f2[4 * ri + q + PAD, pl.ds(at, 1), :], (8, 128))
                if ok is not None:
                    own = own * ok.astype(jnp.float32)
                t = jnp.zeros((8, 128), jnp.float32)
                want = sub8 // 2 - m4
                for s in range(-3, 4):
                    t = jnp.where(want == s, own if s == 0 else pltpu.roll(own, (-s) % 128, 1), t)
                parts.append(t)
            for r in (2 * q, 2 * q + 1):
                for k in range(3):
                    m2[r + H1, 8 * k:8 * k + 8] = m2[r + H1, 8 * k:8 * k + 8] + parts[k]
        for i in range(2 * NU):
            middle(m2, i % 2, 5 - i)
        recv(7)
        unpack_sides(7, vc, H0)
        for q in range(-2, 10):
            y = m2[q + H1]
            tmp[q + 2, pl.ds(0, 24, stride=2), :] = y
            tmp[q + 2, pl.ds(1, 24, stride=2), :] = y
        for r in range(-4, 20):
            t = tmp[r // 2 + 2, 8:40]
            if 0 <= r < 16:
                vc[r + H0, 0:8] = vc[r + H0, 0:8] + t[0:8]
                vc[r + H0, 8:24] = vb[r + H0, 8:24] + t[8:24]
                vc[r + H0, 24:32] = vc[r + H0, 24:32] + t[24:32]
            else:
                vc[r + H0] = vc[r + H0] + t
        for i in range(2 * NU):
            fine(vc, i % 2, 3 - i)
        out[...] = vc[H0:H0 + 16, 8:24]
        for d in range(8):
            @pl.when(has[d])
            def _(d=d):
                for x in range(NX):
                    copy(x, d, origin(x, d), origin(x, d), OPP[d]).wait_send()
        everyone.wait_send()

    return kernel


def solution(mesh):
    nrad, nax = mesh.shape["rad"], mesh.shape["ax"]
    nd = nrad * nax
    n2 = nrad * 4
    f32 = jnp.float32

    def on_device(charge, density, previous, levels):
        vm = pl.BlockSpec(memory_space=pltpu.VMEM)
        fine = pltpu.VMEM((16 + 2 * H0, 32, 128), f32)
        mid = pltpu.VMEM((8 + 2 * H1, 24, 128), f32)
        pack = pltpu.VMEM((10, 24, 128), f32)
        return pl.pallas_call(
            make_kernel(nrad, nax),
            out_shape=jax.ShapeDtypeStruct(charge.shape, f32),
            in_specs=[pl.BlockSpec(memory_space=pltpu.HBM)] * 4,
            out_specs=vm,
            scratch_shapes=[
                pltpu.VMEM((16, 16, 128), f32),
                pltpu.VMEM((16, 16, 128), f32),
                pltpu.VMEM((16, 16, 128), f32),
                pltpu.SMEM((1, 1, 8), jnp.int32),
                pltpu.SemaphoreType.DMA((4,)),
                fine, fine, fine, fine, fine, fine,
                pltpu.VMEM((6, 24, 32, 128), f32),
                pltpu.VMEM((24, 32, 128), f32),
                pltpu.VMEM((16, 16, 128), f32),
                pltpu.VMEM((12, 48, 128), f32),
                pltpu.VMEM((9, 8, 128), jnp.int32),
                mid, mid, mid, mid,
                pltpu.VMEM((6, 18, 24, 128), f32),
                pltpu.VMEM((18, 24, 128), f32),
                pltpu.VMEM((8, 8, 128), f32),
                pltpu.VMEM((8, 16, 128), f32),
                pltpu.VMEM((12, 32, 128), f32),
                pack, pack, pack,
                pltpu.VMEM((3, 2, 8, 8, 128), f32),
                pltpu.VMEM((3, 2, 12, 8, 128), f32),
                pltpu.VMEM((nd, 8, 128), f32),
                pltpu.VMEM((n2 + 2, nax, 128), f32),
                pltpu.VMEM((6, n2, nax, 128), f32),
                pltpu.VMEM((n2, nax, 128), f32),
                pltpu.VMEM((n2 + 2 * PAD, nax, 128), f32),
                pltpu.SemaphoreType.DMA((NX, 8)),
                pltpu.SemaphoreType.DMA((NX, 8)),
                pltpu.SemaphoreType.DMA,
                pltpu.SemaphoreType.DMA,
            ],
            compiler_params=pltpu.CompilerParams(
                collective_id=0, has_side_effects=True, vmem_limit_bytes=64 * 2**20),
        )(charge, density, previous, levels)

    return jax.shard_map(
        on_device, mesh=mesh,
        in_specs=(P("rad", "ax", None),) * 4,
        out_specs=P("rad", "ax", None), check_vma=False)
```
